32 devices in a mesh: row: 8 (over y, x, core), col: 4 (over z).
Axes of the slice: x: 2, y: 2, z: 4, core: 2. Of those that a mesh axis runs over, the one named last changes fastest.
Arguments:
- features: bfloat16 [16384, 1024], P(('row', 'col')), may hold values from 0 to 4, as said below
- coords: float32 [64, 16384], P(None, ('row', 'col')), may hold values from -1 to 1
Outputs:
- placed: float32 [64, 16384], P(None, ('row', 'col'))
- row_stress: float32 [16384], P(('row', 'col'))
- stress_norm: float32 [], replicated
The draws below stay inside these ranges and needn't reach their ends.
Inputs may be any that keep to these rules, and one draw needn't show every extreme that they name: `features`: every molecule has at least one nonzero feature.
All inputs are finite; a program needn't handle non-finite values.
Results may differ from the reference program's by a relative error of at most 0.0003.
Values may be sent and summed in bfloat16 or wider, within the bound.
A program may use at most 192 MiB of HBM per device.

```python
import math
import jax
import jax.numpy as jnp
from jax import lax

DIM = 64
FEAT = 1024
ITERS = 2
MOLS = 16384


def draw_features(key, part):
    key_level = jax.random.fold_in(key, 11)
    key_ticket = jax.random.fold_in(key, 12)
    key_value = jax.random.fold_in(key, 13)
    level = jax.random.randint(key_level, (MOLS, 1), 40, 400)
    ticket = jax.random.randint(key_ticket, (MOLS, FEAT), 0, 1000)
    column = lax.broadcasted_iota(jnp.int32, (MOLS, FEAT), 1)
    own_column = lax.broadcasted_iota(jnp.int32, (MOLS, FEAT), 0) * 7 % FEAT
    present = (ticket < level) | (column == own_column)
    value = jnp.exp(jax.random.uniform(key_value, (MOLS, FEAT), jnp.float32, math.log(0.1), 0.0))
    return jnp.where(present, value, 0.0).astype(jnp.bfloat16)


def draw_coords(key, part):
    position = lax.broadcasted_iota(jnp.float32, (DIM, MOLS), 1) / MOLS
    spread = 0.05 * (1.0 + 2.0 * position)
    base = jnp.clip(jax.random.normal(jax.random.fold_in(key, 22), (DIM, MOLS), jnp.float32), -6.0, 6.0)
    return (base * spread).astype(jnp.float32)


def setup_inputs(seed: int = 0) -> dict:
    keys = jax.random.split(jax.random.key(seed), 3)
    return {
        "features": draw_features(jax.random.fold_in(keys[2], 71), 0),
        "coords": draw_coords(jax.random.fold_in(keys[2], 71), 0),
    }


FLOOR = 0.25
EXACT = lax.Precision.HIGHEST

def reference(features, coords):
    block_len = min(1024, MOLS)
    block_count = MOLS // block_len
    values = features.astype(jnp.float32)
    feat_sq = lax.optimization_barrier(jnp.sum(values * values, axis=1))
    value_blocks = values.reshape(block_count, block_len, FEAT)
    sq_blocks = feat_sq.reshape(block_count, block_len)

    def tanimoto(value_blk, sq_blk):
        common = jnp.dot(value_blk, values.T, precision=EXACT, preferred_element_type=jnp.float32)
        return 1.0 - common / (sq_blk[:, None] + feat_sq[None, :] - common)
    current = coords
    row_stress = jnp.zeros((MOLS,), jnp.float32)
    dissim_total = jnp.zeros((), jnp.float32)
    for sweep in range(ITERS):
        sq_norms = lax.optimization_barrier(jnp.sum(current * current, axis=0))
        x_blocks = jnp.moveaxis(current.reshape(DIM, block_count, block_len), 1, 0)
        norm_blocks = sq_norms.reshape(block_count, block_len)

        def one_block(inputs):
            value_blk, sq_blk, x_blk, norm_blk = inputs
            dissim = tanimoto(value_blk, sq_blk)
            inner = lax.dot_general(x_blk, current, (((0,), (0,)), ((), ())), precision=EXACT, preferred_element_type=jnp.float32)
            distance = jnp.sqrt(jnp.maximum(norm_blk[:, None] + sq_norms[None, :] - 2.0 * inner, FLOOR * FLOOR))
            ratios = dissim / distance
            pulled = lax.dot_general(current, ratios, (((1,), (1,)), ((), ())), precision=EXACT, preferred_element_type=jnp.float32)
            pull_terms = x_blk * lax.optimization_barrier(jnp.sum(ratios, axis=1))[None, :] - pulled
            stress = lax.optimization_barrier(jnp.sum(jnp.square(dissim - distance), axis=1))
            return (pull_terms, stress, jnp.sum(dissim * dissim))
        pull_terms, stress, dis_squares = lax.map(one_block, (value_blocks, sq_blocks, x_blocks, norm_blocks))
        current = jnp.moveaxis(pull_terms, 0, 1).reshape(DIM, MOLS) / MOLS
        row_stress = stress.reshape(MOLS) / MOLS
        dissim_total = jnp.sum(dis_squares)
    stress_norm = MOLS * jnp.sum(row_stress) / dissim_total
    return (current, row_stress, stress_norm)
```

```python
import functools

import jax
import jax.numpy as jnp
from jax import lax
from jax.experimental import pallas as pl
from jax.experimental.pallas import tpu as pltpu
from jax.sharding import PartitionSpec as P

ITERS = 2
FLOOR = 0.25
AUX = 72


def halves(x):
    high = lax.reduce_precision(x, 8, 7)
    low = lax.reduce_precision(x - high, 8, 7)
    return high, low


def operands(high, low, norms):
    dim, length = high.shape
    left = jnp.concatenate([-2.0 * high, -2.0 * high, -2.0 * low, -2.0 * low], axis=0).T
    right = jnp.concatenate([high, low, high, low], axis=0)
    ones = jnp.ones((dim, length), jnp.float32)
    weights = jnp.concatenate([high, low, ones, jnp.zeros_like(ones)], axis=0).T
    return left.astype(jnp.bfloat16), right.astype(jnp.bfloat16), weights.astype(jnp.bfloat16)


def guttman_chunk(dissim, left, right, weights, row_norm, col_norm):
    cross = jnp.dot(left, right, preferred_element_type=jnp.float32)
    dist_sq = jnp.maximum((row_norm + col_norm) + cross, FLOOR * FLOOR)
    inverse = lax.rsqrt(dist_sq)
    ratio = dissim * inverse
    high = ratio.astype(jnp.bfloat16)
    low = (ratio - high.astype(jnp.float32)).astype(jnp.bfloat16)
    moved = jnp.dot(high, weights, preferred_element_type=jnp.float32)
    moved += jnp.dot(low, weights, preferred_element_type=jnp.float32)
    return moved, dist_sq * inverse


def lanes_sum(values):
    total = values[:, :128]
    for at in range(128, values.shape[1], 128):
        total += values[:, at : at + 128]
    return total


def pull_of(moved, x_rows):
    dim = x_rows.shape[1]
    row_sum = moved[:, 2 * dim : 2 * dim + 1]
    return x_rows * row_sum - (moved[:, :dim] + moved[:, dim : 2 * dim])


def first_kernel(chunk, rows_ref, cols_ref, row_sq_ref, col_sq_ref, left_ref, right_ref, weights_ref,
                 row_norm_ref, col_norm_ref, x_ref, dissim_ref, pull_ref, square_ref):
    tile, cols_len = dissim_ref.shape
    rows = rows_ref[...]
    left = left_ref[...]
    row_sq = row_sq_ref[...]
    row_norm = row_norm_ref[...]
    moved = jnp.zeros((tile, weights_ref.shape[1]), jnp.float32)
    squares = jnp.zeros((tile, 128), jnp.float32)
    for start in range(0, cols_len, chunk):
        at = slice(start, start + chunk)
        common = lax.dot_general(
            rows, cols_ref[at, :], (((1,), (1,)), ((), ())), preferred_element_type=jnp.float32
        )
        dissim = 1.0 - common / ((row_sq + col_sq_ref[:, at]) - common)
        dissim_ref[:, at] = dissim
        squares += lanes_sum(dissim * dissim)
        part, _ = guttman_chunk(
            dissim, left, right_ref[:, at], weights_ref[at, :], row_norm, col_norm_ref[:, at]
        )
        moved += part
    pull_ref[...] = pull_of(moved, x_ref[...]).T
    square_ref[...] = jnp.sum(squares.reshape(tile // 8, 8, 128), axis=0)[None]


def later_kernel(chunk, dissim_ref, left_ref, right_ref, weights_ref, row_norm_ref, col_norm_ref, x_ref,
                 pull_ref):
    tile, cols_len = dissim_ref.shape
    dim = x_ref.shape[1]
    left = left_ref[...]
    row_norm = row_norm_ref[...]
    moved = jnp.zeros((tile, weights_ref.shape[1]), jnp.float32)
    misfit = jnp.zeros((tile, 128), jnp.float32)
    for start in range(0, cols_len, chunk):
        at = slice(start, start + chunk)
        dissim = dissim_ref[:, at]
        part, dist = guttman_chunk(
            dissim, left, right_ref[:, at], weights_ref[at, :], row_norm, col_norm_ref[:, at]
        )
        gap = dissim - dist
        misfit += lanes_sum(gap * gap)
        moved += part
    stress = jnp.sum(misfit, axis=1, keepdims=True)
    pull_ref[:dim, :] = pull_of(moved, x_ref[...]).T
    pull_ref[dim:, :] = jnp.broadcast_to(stress, (tile, 128)).T[: AUX - dim]


def on_device(features, coords):
    rows_n = lax.axis_size("row")
    cols_n = lax.axis_size("col")
    dim, share_len = coords.shape
    feat = features.shape[1]
    row_len = share_len * cols_n
    col_len = share_len * rows_n
    molecules = row_len * rows_n
    tile = 256
    chunk = 512
    steps = row_len // tile
    params = pltpu.CompilerParams(vmem_limit_bytes=56 * 1024 * 1024)

    by_row = lambda width: pl.BlockSpec((tile, width), lambda i: (i, 0))
    whole = lambda *shape: pl.BlockSpec(shape, lambda i: (0, 0))

    feature_rows = lax.all_gather(features, "col", axis=0, tiled=True)
    feature_cols = lax.all_gather(features, "row", axis=0, tiled=True)
    wide = features.astype(jnp.float32)
    share_sq = jnp.sum(wide * wide, axis=1)
    zeros = jnp.zeros((AUX - dim - 1, share_len), jnp.float32)

    def spread(current, extra):
        packed = jnp.concatenate([current, extra[None, :], zeros], axis=0)
        return (
            lax.all_gather(packed, "col", axis=1, tiled=True),
            lax.all_gather(packed, "row", axis=1, tiled=True),
        )

    def prepare(rows_aux, cols_aux):
        row_high, row_low = halves(rows_aux[:dim])
        col_high, col_low = halves(cols_aux[:dim])
        row_hat = row_high + row_low
        col_hat = col_high + col_low
        row_norm = jnp.sum(row_hat * row_hat, axis=0)[:, None]
        col_norm = jnp.sum(col_hat * col_hat, axis=0)[None, :]
        left, _, _ = operands(row_high, row_low, row_norm)
        _, right, weights = operands(col_high, col_low, col_norm)
        return left, right, weights, row_norm, col_norm, rows_aux[:dim].T

    guttman_specs = [
        by_row(4 * dim),
        whole(4 * dim, col_len),
        whole(col_len, 4 * dim),
        by_row(1),
        whole(1, col_len),
        by_row(dim),
    ]

    rows_aux, cols_aux = spread(coords, share_sq)
    dissim, pull, squares = pl.pallas_call(
        functools.partial(first_kernel, chunk),
        grid=(steps,),
        in_specs=[by_row(feat), whole(col_len, feat), by_row(1), whole(1, col_len)] + guttman_specs,
        out_specs=[
            by_row(col_len),
            pl.BlockSpec((dim, tile), lambda i: (0, i)),
            pl.BlockSpec((1, 8, 128), lambda i: (i, 0, 0)),
        ],
        out_shape=[
            jax.ShapeDtypeStruct((row_len, col_len), jnp.float32),
            jax.ShapeDtypeStruct((dim, row_len), jnp.float32),
            jax.ShapeDtypeStruct((steps, 8, 128), jnp.float32),
        ],
        compiler_params=params,
    )(
        feature_rows,
        feature_cols,
        rows_aux[dim][:, None],
        cols_aux[dim][None, :],
        *prepare(rows_aux, cols_aux),
    )
    dissim_sq = jnp.sum(squares)
    current = lax.psum_scatter(pull, "col", scatter_dimension=1, tiled=True) / molecules
    for sweep in range(1, ITERS):
        rows_aux = lax.all_gather(current, "col", axis=1, tiled=True)
        cols_aux = lax.all_gather(current, "row", axis=1, tiled=True)
        pull = pl.pallas_call(
            functools.partial(later_kernel, chunk),
            grid=(steps,),
            in_specs=[by_row(col_len)] + guttman_specs,
            out_specs=pl.BlockSpec((AUX, tile), lambda i: (0, i)),
            out_shape=jax.ShapeDtypeStruct((AUX, row_len), jnp.float32),
            compiler_params=params,
        )(dissim, *prepare(rows_aux, cols_aux))
        reduced = lax.psum_scatter(pull, "col", scatter_dimension=1, tiled=True) / molecules
        current = reduced[:dim]
        row_stress = reduced[dim]
    stress_total, dissim_total = lax.psum((jnp.sum(row_stress), dissim_sq), ("row", "col"))
    stress_norm = molecules * stress_total / dissim_total
    return (current, row_stress, stress_norm)


def solution(mesh):
    return jax.shard_map(
        on_device,
        mesh=mesh,
        in_specs=(P(("row", "col"), None), P(None, ("row", "col"))),
        out_specs=(P(None, ("row", "col")), P(("row", "col")), P()),
        check_vma=False,
    )
```

```python
import functools

import jax
import jax.numpy as jnp
from jax import lax
from jax.experimental import pallas as pl
from jax.experimental.pallas import tpu as pltpu
from jax.sharding import PartitionSpec as P

ITERS = 2
FLOOR = 0.25
LANES = 128
MESH = pl.DeviceIdType.MESH


def halves(x):
    high = lax.reduce_precision(x, 8, 7)
    return high, lax.reduce_precision(x - high, 8, 7)


def lanes_sum(values):
    total = values[:, :LANES]
    for at in range(LANES, values.shape[1], LANES):
        total += values[:, at : at + LANES]
    return total


def rows_sum(values):
    return jnp.sum(values.reshape(values.shape[0] // 8, 8, LANES), axis=0)


def with_norms(x, extra):
    length, dim = x.shape
    high, low = halves(x)
    hat = high + low
    norm = jnp.sum(hat * hat, axis=1, keepdims=True)
    lane = lax.broadcasted_iota(jnp.int32, (length, LANES - dim), 1)
    tail = jnp.where(lane == 0, norm, jnp.where(lane == 1, extra, 0.0))
    return jnp.concatenate([x, tail], axis=1)


def peers():
    row, col = lax.axis_index("row"), lax.axis_index("col")
    rows_n, cols_n = lax.axis_size("row"), lax.axis_size("col")
    along_row = [(k, (lax.rem(row + k, rows_n), col)) for k in range(1, rows_n)]
    along_col = [(k, (row, lax.rem(col + k, cols_n))) for k in range(1, cols_n)]
    return row, col, along_row, along_col


def greet(along_row, along_col):
    barrier = pltpu.get_barrier_semaphore()
    for _, device in along_row + along_col:
        pl.semaphore_signal(barrier, inc=1, device_id=device, device_id_type=MESH)
    pl.semaphore_wait(barrier, len(along_row) + len(along_col))


def send(source, target, sems, k, device):
    copy = pltpu.make_async_remote_copy(
        src_ref=source, dst_ref=target, send_sem=sems.at[0, k], recv_sem=sems.at[1, k],
        device_id=device, device_id_type=MESH,
    )
    copy.start()
    return copy


def gather_kernel(features_ref, aux_ref, frows_ref, fcols_ref, arows_ref, acols_ref, own, fr, fc, ar, ac):
    row, col, along_row, along_col = peers()
    local = []
    for at, (src, dst, place) in enumerate((
        (features_ref, frows_ref, col), (features_ref, fcols_ref, row),
        (aux_ref, arows_ref, col), (aux_ref, acols_ref, row),
    )):
        local.append(pltpu.make_async_copy(src, dst.at[place], own.at[at]))
        local[-1].start()
    greet(along_row, along_col)
    copies = []
    for k, device in along_col:
        copies.append(send(features_ref, frows_ref.at[col], fr, k, device))
    for k, device in along_row:
        copies.append(send(features_ref, fcols_ref.at[row], fc, k, device))
    for k, device in along_col:
        copies.append(send(aux_ref, arows_ref.at[col], ar, k, device))
    for k, device in along_row:
        copies.append(send(aux_ref, acols_ref.at[row], ac, k, device))
    for copy in local + copies:
        copy.wait()


def reduce_shares(pull_ref, inbox, sems, col, along_col, molecules):
    copies = []
    for k, device in along_col:
        copies.append(send(pull_ref.at[device[1]], inbox.at[col], sems, k, device))
    inbox[col] = pull_ref[col]
    for copy in copies:
        copy.wait()
    total = inbox[0]
    for at in range(1, len(along_col) + 1):
        total += inbox[at]
    return total / molecules


def turn_kernel(molecules, dim, pull_ref, arows_ref, acols_ref, inbox, mine, rs, ar, ac):
    row, col, along_row, along_col = peers()
    greet(along_row, along_col)
    total = reduce_shares(pull_ref, inbox, rs, col, along_col, molecules)
    aux = with_norms(total[:, :dim], 0.0)
    mine[...] = aux
    copies = []
    for k, device in along_col:
        copies.append(send(mine, arows_ref.at[col], ar, k, device))
    for k, device in along_row:
        copies.append(send(mine, acols_ref.at[row], ac, k, device))
    arows_ref[col] = aux
    acols_ref[row] = aux
    for copy in copies:
        copy.wait()


def last_kernel(molecules, pull_ref, part_ref, share_ref, total_ref, inbox, rowbox, colbox, mine, rs, sr, sc):
    row, col, along_row, along_col = peers()
    greet(along_row, along_col)
    copies = []
    for k, device in along_row:
        copies.append(send(part_ref, rowbox.at[row], sr, k, device))
    rowbox[row] = part_ref[...]
    for copy in copies:
        copy.wait()
    total = rowbox[0]
    for at in range(1, len(along_row) + 1):
        total += rowbox[at]
    mine[...] = total
    copies = []
    for k, device in along_col:
        copies.append(send(mine, colbox.at[col], sc, k, device))
    colbox[col] = total
    share_ref[...] = reduce_shares(pull_ref, inbox, rs, col, along_col, molecules)
    for copy in copies:
        copy.wait()
    total = colbox[0]
    for at in range(1, len(along_col) + 1):
        total += colbox[at]
    total_ref[...] = total


def prepare(dim, aux_ref, right, weights, lines):
    length = aux_ref.shape[0]
    piece = min(512, length)

    @pl.when(pl.program_id(0) == 0)
    def _():
        for start in range(0, length, piece):
            at = slice(start, start + piece)
            values = aux_ref[at, :]
            high, low = halves(values[:, :dim])
            right[at, :] = jnp.concatenate([high, low, high, low], axis=1).astype(jnp.bfloat16)
            ones = jnp.ones((piece, dim), jnp.float32)
            weights[at, :] = jnp.concatenate([high, low, ones, 0.0 * ones], axis=1).astype(jnp.bfloat16)
            lines[:, at] = values.T[dim : dim + 8]


def tile_kernel(first, chunk, dim, *refs):
    if first:
        rows_ref, cols_ref, arow_ref, acol_ref, dissim_ref, pull_ref, square_ref, right, weights, lines = refs
        rows = rows_ref[...]
    else:
        dissim_ref, arow_ref, acol_ref, pull_ref, square_ref, right, weights, lines = refs
    prepare(dim, acol_ref, right, weights, lines)
    tile, cols_len = dissim_ref.shape
    x = arow_ref[:, :dim]
    high, low = halves(x)
    left = (-2.0 * jnp.concatenate([high, high, low, low], axis=1)).astype(jnp.bfloat16)
    row_norm = arow_ref[:, dim : dim + 1]
    row_sq = arow_ref[:, dim + 1 : dim + 2]
    moved = jnp.zeros((tile, 4 * dim), jnp.float32)
    squares = jnp.zeros((tile, LANES), jnp.float32)
    contract = (((1,), (1,)), ((), ()))
    for start in range(0, cols_len, chunk):
        at = slice(start, start + chunk)
        if first:
            common = lax.dot_general(rows, cols_ref[at, :], contract, preferred_element_type=jnp.float32)
            dissim = 1.0 - common / ((row_sq + lines[1:2, at]) - common)
            dissim_ref[:, at] = dissim
        else:
            dissim = dissim_ref[:, at]
        cross = lax.dot_general(left, right[at, :], contract, preferred_element_type=jnp.float32)
        dist_sq = jnp.maximum((row_norm + lines[0:1, at]) + cross, FLOOR * FLOOR)
        inverse = lax.rsqrt(dist_sq)
        ratio = dissim * inverse
        gap = dissim if first else dissim - dist_sq * inverse
        squares += lanes_sum(gap * gap)
        top = ratio.astype(jnp.bfloat16)
        rest = (ratio - top.astype(jnp.float32)).astype(jnp.bfloat16)
        moved += jnp.dot(top, weights[at, :], preferred_element_type=jnp.float32)
        moved += jnp.dot(rest, weights[at, :], preferred_element_type=jnp.float32)
    pull = x * moved[:, 2 * dim : 2 * dim + 1] - (moved[:, :dim] + moved[:, dim : 2 * dim])
    stress = jnp.sum(squares, axis=1, keepdims=True)
    pull_ref[...] = jnp.concatenate([pull, jnp.broadcast_to(stress, (tile, LANES - dim))], axis=1)
    square_ref[...] = rows_sum(squares)[None]


def on_device(features, coords):
    rows_n = lax.axis_size("row")
    cols_n = lax.axis_size("col")
    dim, share_len = coords.shape
    feat = features.shape[1]
    row_len = share_len * cols_n
    col_len = share_len * rows_n
    molecules = row_len * rows_n
    tile = 256
    chunk = 512
    steps = row_len // tile
    big = 56 * 1024 * 1024
    f32 = jnp.float32
    any_spec = pl.BlockSpec(memory_space=pl.ANY)
    vmem = pl.BlockSpec(memory_space=pltpu.VMEM)
    dma = pltpu.SemaphoreType.DMA

    def shape(*sizes, dtype=f32):
        return jax.ShapeDtypeStruct(sizes, dtype)

    def comm(number):
        return pltpu.CompilerParams(collective_id=number, has_side_effects=True, vmem_limit_bytes=big)

    wide = features.astype(f32)
    aux = with_norms(coords.T, jnp.sum(wide * wide, axis=1, keepdims=True))
    frows, fcols, arows, acols = pl.pallas_call(
        gather_kernel,
        in_specs=[any_spec, any_spec],
        out_specs=[any_spec] * 4,
        out_shape=[
            shape(cols_n, share_len, feat, dtype=features.dtype),
            shape(rows_n, share_len, feat, dtype=features.dtype),
            shape(cols_n, share_len, LANES),
            shape(rows_n, share_len, LANES),
        ],
        scratch_shapes=[dma((4,)), dma((2, cols_n)), dma((2, rows_n)), dma((2, cols_n)), dma((2, rows_n))],
        compiler_params=comm(0),
    )(features, aux)

    by_row = lambda width: pl.BlockSpec((tile, width), lambda i: (i, 0))
    whole = lambda *sizes: pl.BlockSpec(sizes, lambda i: (0, 0))

    def tiles(first, *given):
        specs = [by_row(feat), whole(col_len, feat)] if first else [by_row(col_len)]
        outs = [by_row(LANES), pl.BlockSpec((1, 8, LANES), lambda i: (i, 0, 0))]
        shapes = [shape(row_len, LANES), shape(steps, 8, LANES)]
        if first:
            outs, shapes = [by_row(col_len)] + outs, [shape(row_len, col_len)] + shapes
        return pl.pallas_call(
            functools.partial(tile_kernel, first, chunk, dim),
            grid=(steps,),
            in_specs=specs + [by_row(LANES), whole(col_len, LANES)],
            out_specs=outs,
            out_shape=shapes,
            scratch_shapes=[
                pltpu.VMEM((col_len, 4 * dim), jnp.bfloat16),
                pltpu.VMEM((col_len, 4 * dim), jnp.bfloat16),
                pltpu.VMEM((8, col_len), f32),
            ],
            compiler_params=pltpu.CompilerParams(vmem_limit_bytes=big),
        )(*given)

    dissim, pull, dis_squares = tiles(
        True, frows.reshape(row_len, feat), fcols.reshape(col_len, feat),
        arows.reshape(row_len, LANES), acols.reshape(col_len, LANES),
    )
    inbox = pltpu.VMEM((cols_n, share_len, LANES), f32)
    mine = pltpu.VMEM((share_len, LANES), f32)
    for sweep in range(1, ITERS):
        arows, acols = pl.pallas_call(
            functools.partial(turn_kernel, molecules, dim),
            in_specs=[vmem],
            out_specs=[vmem, vmem],
            out_shape=[shape(cols_n, share_len, LANES), shape(rows_n, share_len, LANES)],
            scratch_shapes=[inbox, mine, dma((2, cols_n)), dma((2, cols_n)), dma((2, rows_n))],
            compiler_params=comm(sweep),
        )(pull.reshape(cols_n, share_len, LANES))
        pull, misfits = tiles(False, dissim, arows.reshape(row_len, LANES), acols.reshape(col_len, LANES))
    parts = jnp.stack([jnp.sum(misfits, axis=0), jnp.sum(dis_squares, axis=0)])
    share, totals = pl.pallas_call(
        functools.partial(last_kernel, molecules),
        in_specs=[vmem, vmem],
        out_specs=[vmem, vmem],
        out_shape=[shape(share_len, LANES), shape(2, 8, LANES)],
        scratch_shapes=[
            inbox, pltpu.VMEM((rows_n, 2, 8, LANES), f32), pltpu.VMEM((cols_n, 2, 8, LANES), f32),
            pltpu.VMEM((2, 8, LANES), f32), dma((2, cols_n)), dma((2, rows_n)), dma((2, cols_n)),
        ],
        compiler_params=comm(ITERS),
    )(pull.reshape(cols_n, share_len, LANES), parts)
    totals = jnp.sum(totals, axis=(1, 2))
    return (share[:, :dim].T, share[:, dim], totals[0] / totals[1])


def solution(mesh):
    return jax.shard_map(
        on_device,
        mesh=mesh,
        in_specs=(P(("row", "col"), None), P(None, ("row", "col"))),
        out_specs=(P(None, ("row", "col")), P(("row", "col")), P()),
        check_vma=False,
    )
```

```python
import functools

import jax
import jax.numpy as jnp
from jax import lax
from jax.experimental import pallas as pl
from jax.experimental.pallas import tpu as pltpu
from jax.sharding import PartitionSpec as P

ITERS = 2
FLOOR = 0.25
LANES = 128
MESH = pl.DeviceIdType.MESH


def halves(x):
    high = lax.reduce_precision(x, 8, 7)
    return high, lax.reduce_precision(x - high, 8, 7)


def lanes_sum(values):
    total = values[:, :LANES]
    for at in range(LANES, values.shape[1], LANES):
        total += values[:, at : at + LANES]
    return total


def rows_sum(values):
    return jnp.sum(values.reshape(values.shape[0] // 8, 8, LANES), axis=0)


def with_norms(x, extra):
    length, dim = x.shape
    high, low = halves(x)
    hat = high + low
    norm = jnp.sum(hat * hat, axis=1, keepdims=True)
    lane = lax.broadcasted_iota(jnp.int32, (length, LANES - dim), 1)
    tail = jnp.where(lane == 0, norm, jnp.where(lane == 1, extra, 0.0))
    return jnp.concatenate([x, tail], axis=1)


def peers():
    row, col = lax.axis_index("row"), lax.axis_index("col")
    rows_n, cols_n = lax.axis_size("row"), lax.axis_size("col")
    along_row = [(k, (lax.rem(row + k, rows_n), col)) for k in range(1, rows_n)]
    along_col = [(k, (row, lax.rem(col + k, cols_n))) for k in range(1, cols_n)]
    return row, col, along_row, along_col


def greet(along_row, along_col):
    barrier = pltpu.get_barrier_semaphore()
    for _, device in along_row + along_col:
        pl.semaphore_signal(barrier, inc=1, device_id=device, device_id_type=MESH)
    pl.semaphore_wait(barrier, len(along_row) + len(along_col))


def send(source, target, sems, k, device):
    copy = pltpu.make_async_remote_copy(
        src_ref=source, dst_ref=target, send_sem=sems.at[0, k], recv_sem=sems.at[1, k],
        device_id=device, device_id_type=MESH,
    )
    copy.start()
    return copy


def link(source, target, sems, k, device):
    return pltpu.make_async_remote_copy(
        src_ref=source, dst_ref=target, send_sem=sems.at[0, k], recv_sem=sems.at[1, k],
        device_id=device, device_id_type=MESH,
    )


def spread(row, col, arrays):
    rows_n, cols_n = lax.axis_size("row"), lax.axis_size("col")
    chips = rows_n // 2
    chip, core = row // 2, lax.rem(row, 2)
    twin = (2 * chip + 1 - core, col)

    def inside(at):
        return (at >= 0) & (at < cols_n)

    def relay(array, t, step):
        source, by_col, _, sems = array
        slot = col - step * t
        return link(source if t == 0 else by_col.at[slot], by_col.at[slot],
                    sems[0] if step == 1 else sems[1], t, (row, col + step))

    def sends(t, step, act):
        @pl.when(inside(col - step * t) & inside(col + step))
        def _():
            for array in arrays:
                act(relay(array, t, step))

    def arrival(t, step):
        @pl.when(inside(col - step * (t + 1)))
        def _():
            for _, by_col, _, sems in arrays:
                slot = by_col.at[col - step * (t + 1)]
                link(slot, slot, sems[0] if step == 1 else sems[1], t, (row, col - step)).wait_recv()

    def cross(array, k):
        source, _, by_row, sems = array
        return link(source, by_row.at[row], sems[2], k, (2 * lax.rem(chip + k, chips) + core, col))

    def pass_on(array, k):
        source, _, by_row, sems = array
        slot = 2 * lax.rem(chip + chips - k, chips) + core
        return link(source if k == 0 else by_row.at[slot], by_row.at[slot], sems[3], k, twin)

    def forward(k):
        for array in arrays:
            cross(array, k).wait_recv()
            pass_on(array, k).start()

    for step in (1, -1):
        sends(0, step, lambda copy: copy.start())
    for k in range(1, chips):
        for array in arrays:
            cross(array, k).start()
    for array in arrays:
        pass_on(array, 0).start()
    for t in range(cols_n - 1):
        for step in (1, -1):
            arrival(t, step)
            if t + 1 < cols_n - 1:
                sends(t + 1, step, lambda copy: copy.start())
        if t + 1 < chips:
            forward(t + 1)
    for k in range(cols_n, chips):
        forward(k)
    for t in range(cols_n - 1):
        for step in (1, -1):
            sends(t, step, lambda copy: copy.wait_send())
    for array in arrays:
        for k in range(1, chips):
            cross(array, k).wait_send()
        for k in range(chips):
            pass_on(array, k).wait()


def gather_kernel(features_ref, aux_ref, frows_ref, fcols_ref, arows_ref, acols_ref, own, *sems):
    row, col, along_row, along_col = peers()
    local = []
    for at, (src, dst, place) in enumerate((
        (features_ref, frows_ref, col), (features_ref, fcols_ref, row),
        (aux_ref, arows_ref, col), (aux_ref, acols_ref, row),
    )):
        local.append(pltpu.make_async_copy(src, dst.at[place], own.at[at]))
        local[-1].start()
    greet(along_row, along_col)
    spread(row, col, [(features_ref, frows_ref, fcols_ref, sems[:4]), (aux_ref, arows_ref, acols_ref, sems[4:])])
    for copy in local:
        copy.wait()


def reduce_shares(pull_ref, inbox, sems, col, along_col, molecules):
    copies = []
    for k, device in along_col:
        copies.append(send(pull_ref.at[device[1]], inbox.at[col], sems, k, device))
    inbox[col] = pull_ref[col]
    for copy in copies:
        copy.wait()
    total = inbox[0]
    for at in range(1, len(along_col) + 1):
        total += inbox[at]
    return total / molecules


def turn_kernel(molecules, dim, pull_ref, arows_ref, acols_ref, inbox, mine, rs, *sems):
    row, col, along_row, along_col = peers()
    greet(along_row, along_col)
    total = reduce_shares(pull_ref, inbox, rs, col, along_col, molecules)
    aux = with_norms(total[:, :dim], 0.0)
    mine[...] = aux
    arows_ref[col] = aux
    acols_ref[row] = aux
    spread(row, col, [(mine, arows_ref, acols_ref, sems)])


def last_kernel(molecules, pull_ref, part_ref, share_ref, total_ref, inbox, rowbox, colbox, mine, rs, sr, sc):
    row, col, along_row, along_col = peers()
    greet(along_row, along_col)
    copies = []
    for k, device in along_row:
        copies.append(send(part_ref, rowbox.at[row], sr, k, device))
    rowbox[row] = part_ref[...]
    for copy in copies:
        copy.wait()
    total = rowbox[0]
    for at in range(1, len(along_row) + 1):
        total += rowbox[at]
    mine[...] = total
    copies = []
    for k, device in along_col:
        copies.append(send(mine, colbox.at[col], sc, k, device))
    colbox[col] = total
    share_ref[...] = reduce_shares(pull_ref, inbox, rs, col, along_col, molecules)
    for copy in copies:
        copy.wait()
    total = colbox[0]
    for at in range(1, len(along_col) + 1):
        total += colbox[at]
    total_ref[...] = total


def prepare(dim, aux_ref, right, weights, lines):
    length = aux_ref.shape[0]
    piece = min(512, length)

    @pl.when(pl.program_id(0) == 0)
    def _():
        for start in range(0, length, piece):
            at = slice(start, start + piece)
            values = aux_ref[at, :]
            high, low = halves(values[:, :dim])
            right[at, :] = jnp.concatenate([high, low, high, low], axis=1).astype(jnp.bfloat16)
            ones = jnp.ones((piece, dim), jnp.float32)
            weights[at, :] = jnp.concatenate([high, low, ones, 0.0 * ones], axis=1).astype(jnp.bfloat16)
            lines[:, at] = values.T[dim : dim + 8]


def tile_kernel(first, chunk, dim, *refs):
    if first:
        rows_ref, cols_ref, arow_ref, acol_ref, dissim_ref, pull_ref, square_ref, right, weights, lines = refs
        rows = rows_ref[...]
    else:
        dissim_ref, arow_ref, acol_ref, pull_ref, square_ref, right, weights, lines = refs
    prepare(dim, acol_ref, right, weights, lines)
    tile, cols_len = dissim_ref.shape
    x = arow_ref[:, :dim]
    high, low = halves(x)
    left = (-2.0 * jnp.concatenate([high, high, low, low], axis=1)).astype(jnp.bfloat16)
    row_norm = arow_ref[:, dim : dim + 1]
    row_sq = arow_ref[:, dim + 1 : dim + 2]
    moved = jnp.zeros((tile, 4 * dim), jnp.float32)
    squares = jnp.zeros((tile, LANES), jnp.float32)
    contract = (((1,), (1,)), ((), ()))
    for start in range(0, cols_len, chunk):
        at = slice(start, start + chunk)
        if first:
            common = lax.dot_general(rows, cols_ref[at, :], contract, preferred_element_type=jnp.float32)
            dissim = 1.0 - common / ((row_sq + lines[1:2, at]) - common)
            dissim_ref[:, at] = dissim
        else:
            dissim = dissim_ref[:, at]
        cross = lax.dot_general(left, right[at, :], contract, preferred_element_type=jnp.float32)
        dist_sq = jnp.maximum((row_norm + lines[0:1, at]) + cross, FLOOR * FLOOR)
        inverse = lax.rsqrt(dist_sq)
        ratio = dissim * inverse
        gap = dissim if first else dissim - dist_sq * inverse
        squares += lanes_sum(gap * gap)
        top = ratio.astype(jnp.bfloat16)
        rest = (ratio - top.astype(jnp.float32)).astype(jnp.bfloat16)
        moved += jnp.dot(top, weights[at, :], preferred_element_type=jnp.float32)
        moved += jnp.dot(rest, weights[at, :], preferred_element_type=jnp.float32)
    pull = x * moved[:, 2 * dim : 2 * dim + 1] - (moved[:, :dim] + moved[:, dim : 2 * dim])
    stress = jnp.sum(squares, axis=1, keepdims=True)
    pull_ref[...] = jnp.concatenate([pull, jnp.broadcast_to(stress, (tile, LANES - dim))], axis=1)
    square_ref[...] = rows_sum(squares)[None]


def on_device(features, coords):
    rows_n = lax.axis_size("row")
    cols_n = lax.axis_size("col")
    dim, share_len = coords.shape
    feat = features.shape[1]
    row_len = share_len * cols_n
    col_len = share_len * rows_n
    molecules = row_len * rows_n
    tile = 256
    chunk = 512
    steps = row_len // tile
    big = 56 * 1024 * 1024
    f32 = jnp.float32
    any_spec = pl.BlockSpec(memory_space=pl.ANY)
    vmem = pl.BlockSpec(memory_space=pltpu.VMEM)
    dma = pltpu.SemaphoreType.DMA
    spread_sems = [dma((2, cols_n))] * 2 + [dma((2, rows_n // 2))] * 2

    def shape(*sizes, dtype=f32):
        return jax.ShapeDtypeStruct(sizes, dtype)

    def comm(number):
        return pltpu.CompilerParams(collective_id=number, has_side_effects=True, vmem_limit_bytes=big)

    wide = features.astype(f32)
    aux = with_norms(coords.T, jnp.sum(wide * wide, axis=1, keepdims=True))
    frows, fcols, arows, acols = pl.pallas_call(
        gather_kernel,
        in_specs=[any_spec, any_spec],
        out_specs=[any_spec] * 4,
        out_shape=[
            shape(cols_n, share_len, feat, dtype=features.dtype),
            shape(rows_n, share_len, feat, dtype=features.dtype),
            shape(cols_n, share_len, LANES),
            shape(rows_n, share_len, LANES),
        ],
        scratch_shapes=[dma((4,))] + spread_sems + spread_sems,
        compiler_params=comm(0),
    )(features, aux)

    by_row = lambda width: pl.BlockSpec((tile, width), lambda i: (i, 0))
    whole = lambda *sizes: pl.BlockSpec(sizes, lambda i: (0, 0))

    def tiles(first, *given):
        specs = [by_row(feat), whole(col_len, feat)] if first else [by_row(col_len)]
        outs = [by_row(LANES), pl.BlockSpec((1, 8, LANES), lambda i: (i, 0, 0))]
        shapes = [shape(row_len, LANES), shape(steps, 8, LANES)]
        if first:
            outs, shapes = [by_row(col_len)] + outs, [shape(row_len, col_len)] + shapes
        return pl.pallas_call(
            functools.partial(tile_kernel, first, chunk, dim),
            grid=(steps,),
            in_specs=specs + [by_row(LANES), whole(col_len, LANES)],
            out_specs=outs,
            out_shape=shapes,
            scratch_shapes=[
                pltpu.VMEM((col_len, 4 * dim), jnp.bfloat16),
                pltpu.VMEM((col_len, 4 * dim), jnp.bfloat16),
                pltpu.VMEM((8, col_len), f32),
            ],
            compiler_params=pltpu.CompilerParams(vmem_limit_bytes=big),
        )(*given)

    dissim, pull, dis_squares = tiles(
        True, frows.reshape(row_len, feat), fcols.reshape(col_len, feat),
        arows.reshape(row_len, LANES), acols.reshape(col_len, LANES),
    )
    inbox = pltpu.VMEM((cols_n, share_len, LANES), f32)
    mine = pltpu.VMEM((share_len, LANES), f32)
    for sweep in range(1, ITERS):
        arows, acols = pl.pallas_call(
            functools.partial(turn_kernel, molecules, dim),
            in_specs=[vmem],
            out_specs=[vmem, vmem],
            out_shape=[shape(cols_n, share_len, LANES), shape(rows_n, share_len, LANES)],
            scratch_shapes=[inbox, mine, dma((2, cols_n))] + spread_sems,
            compiler_params=comm(sweep),
        )(pull.reshape(cols_n, share_len, LANES))
        pull, misfits = tiles(False, dissim, arows.reshape(row_len, LANES), acols.reshape(col_len, LANES))
    parts = jnp.stack([jnp.sum(misfits, axis=0), jnp.sum(dis_squares, axis=0)])
    share, totals = pl.pallas_call(
        functools.partial(last_kernel, molecules),
        in_specs=[vmem, vmem],
        out_specs=[vmem, vmem],
        out_shape=[shape(share_len, LANES), shape(2, 8, LANES)],
        scratch_shapes=[
            inbox, pltpu.VMEM((rows_n, 2, 8, LANES), f32), pltpu.VMEM((cols_n, 2, 8, LANES), f32),
            pltpu.VMEM((2, 8, LANES), f32), dma((2, cols_n)), dma((2, rows_n)), dma((2, cols_n)),
        ],
        compiler_params=comm(ITERS),
    )(pull.reshape(cols_n, share_len, LANES), parts)
    totals = jnp.sum(totals, axis=(1, 2))
    return (share[:, :dim].T, share[:, dim], totals[0] / totals[1])


def solution(mesh):
    return jax.shard_map(
        on_device,
        mesh=mesh,
        in_specs=(P(("row", "col"), None), P(None, ("row", "col"))),
        out_specs=(P(None, ("row", "col")), P(("row", "col")), P()),
        check_vma=False,
    )
```

```python
import functools

import jax
import jax.numpy as jnp
from jax import lax
from jax.experimental import pallas as pl
from jax.experimental.pallas import tpu as pltpu
from jax.sharding import PartitionSpec as P

ITERS = 2
FLOOR = 0.25
LANES = 128
MESH = pl.DeviceIdType.MESH


def halves(x):
    high = lax.reduce_precision(x, 8, 7)
    return high, lax.reduce_precision(x - high, 8, 7)


def lanes_sum(values):
    total = values[:, :LANES]
    for at in range(LANES, values.shape[1], LANES):
        total += values[:, at : at + LANES]
    return total


def rows_sum(values):
    return jnp.sum(values.reshape(values.shape[0] // 8, 8, LANES), axis=0)


def with_norms(x, extra):
    length, dim = x.shape
    high, low = halves(x)
    hat = high + low
    norm = jnp.sum(hat * hat, axis=1, keepdims=True)
    lane = lax.broadcasted_iota(jnp.int32, (length, LANES - dim), 1)
    tail = jnp.where(lane == 0, norm, jnp.where(lane == 1, extra, 0.0))
    return jnp.concatenate([x, tail], axis=1)


def peers():
    row, col = lax.axis_index("row"), lax.axis_index("col")
    rows_n, cols_n = lax.axis_size("row"), lax.axis_size("col")
    along_row = [(k, (lax.rem(row + k, rows_n), col)) for k in range(1, rows_n)]
    along_col = [(k, (row, lax.rem(col + k, cols_n))) for k in range(1, cols_n)]
    return row, col, along_row, along_col


def greet(along_row, along_col):
    barrier = pltpu.get_barrier_semaphore()
    for _, device in along_row + along_col:
        pl.semaphore_signal(barrier, inc=1, device_id=device, device_id_type=MESH)
    pl.semaphore_wait(barrier, len(along_row) + len(along_col))


def send(source, target, sems, k, device):
    copy = pltpu.make_async_remote_copy(
        src_ref=source, dst_ref=target, send_sem=sems.at[0, k], recv_sem=sems.at[1, k],
        device_id=device, device_id_type=MESH,
    )
    copy.start()
    return copy


def link(source, target, sems, k, device):
    return pltpu.make_async_remote_copy(
        src_ref=source, dst_ref=target, send_sem=sems.at[0, k], recv_sem=sems.at[1, k],
        device_id=device, device_id_type=MESH,
    )


def spread(row, col, arrays):
    rows_n, cols_n = lax.axis_size("row"), lax.axis_size("col")
    chips = rows_n // 2
    chip, core = row // 2, lax.rem(row, 2)
    twin = (2 * chip + 1 - core, col)

    def inside(at):
        return (at >= 0) & (at < cols_n)

    def relay(array, t, step):
        source, by_col, _, sems = array
        slot = col - step * t
        return link(source if t == 0 else by_col.at[slot], by_col.at[slot],
                    sems[0] if step == 1 else sems[1], t, (row, col + step))

    def sends(t, step, act):
        @pl.when(inside(col - step * t) & inside(col + step))
        def _():
            for array in arrays:
                act(relay(array, t, step))

    def arrival(t, step):
        @pl.when(inside(col - step * (t + 1)))
        def _():
            for _, by_col, _, sems in arrays:
                slot = by_col.at[col - step * (t + 1)]
                link(slot, slot, sems[0] if step == 1 else sems[1], t, (row, col - step)).wait_recv()

    def cross(array, k):
        source, _, by_row, sems = array
        return link(source, by_row.at[row], sems[2], k, (2 * lax.rem(chip + k, chips) + core, col))

    def pass_on(array, k):
        source, _, by_row, sems = array
        slot = 2 * lax.rem(chip + chips - k, chips) + core
        return link(source if k == 0 else by_row.at[slot], by_row.at[slot], sems[3], k, twin)

    def forward(k):
        for array in arrays:
            cross(array, k).wait_recv()
            pass_on(array, k).start()

    for step in (1, -1):
        sends(0, step, lambda copy: copy.start())
    for k in range(1, chips):
        for array in arrays:
            cross(array, k).start()
    for array in arrays:
        pass_on(array, 0).start()
    for t in range(cols_n - 1):
        for step in (1, -1):
            arrival(t, step)
            if t + 1 < cols_n - 1:
                sends(t + 1, step, lambda copy: copy.start())
        if t + 1 < chips:
            forward(t + 1)
    for k in range(cols_n, chips):
        forward(k)
    for t in range(cols_n - 1):
        for step in (1, -1):
            sends(t, step, lambda copy: copy.wait_send())
    for array in arrays:
        for k in range(1, chips):
            cross(array, k).wait_send()
        for k in range(chips):
            pass_on(array, k).wait()


def gather_kernel(features_ref, aux_ref, frows_ref, fcols_ref, arows_ref, acols_ref, own, *sems):
    row, col, along_row, along_col = peers()
    local = []
    for at, (src, dst, place) in enumerate((
        (features_ref, frows_ref, col), (features_ref, fcols_ref, row),
        (aux_ref, arows_ref, col), (aux_ref, acols_ref, row),
    )):
        local.append(pltpu.make_async_copy(src, dst.at[place], own.at[at]))
        local[-1].start()
    greet(along_row, along_col)
    spread(row, col, [(features_ref, frows_ref, fcols_ref, sems[:4]), (aux_ref, arows_ref, acols_ref, sems[4:])])
    for copy in local:
        copy.wait()


def reduce_shares(pull_ref, inbox, sems, col, along_col, molecules):
    length = inbox.shape[2]
    share_of = lambda at: pl.ds(pl.multiple_of(at * length, LANES), length)
    copies = []
    for k, device in along_col:
        copies.append(send(pull_ref.at[:, share_of(device[1])], inbox.at[col], sems, k, device))
    inbox[col] = pull_ref[:, share_of(col)]
    for copy in copies:
        copy.wait()
    total = inbox[0]
    for at in range(1, len(along_col) + 1):
        total += inbox[at]
    return total / molecules


def turn_kernel(molecules, dim, pull_ref, arows_ref, acols_ref, inbox, rowsbox, colsbox, mine, rs, *sems):
    row, col, along_row, along_col = peers()
    greet(along_row, along_col)
    total = reduce_shares(pull_ref, inbox, rs, col, along_col, molecules)
    used, length = mine.shape
    mine[...] = with_norms(total[:dim].T, 0.0).T[:used]
    rowsbox[col] = mine[...]
    colsbox[row] = mine[...]
    spread(row, col, [(mine, rowsbox, colsbox, sems)])
    pad = jnp.zeros((LANES - used, length), jnp.float32)
    for box, out in ((rowsbox, arows_ref), (colsbox, acols_ref)):
        for at in range(box.shape[0]):
            out[at] = jnp.concatenate([box[at], pad], axis=0).T


def last_kernel(molecules, pull_ref, part_ref, share_ref, total_ref, inbox, rowbox, colbox, mine, rs, sr, sc):
    row, col, along_row, along_col = peers()
    greet(along_row, along_col)
    copies = []
    for k, device in along_row:
        copies.append(send(part_ref, rowbox.at[row], sr, k, device))
    rowbox[row] = part_ref[...]
    for copy in copies:
        copy.wait()
    total = rowbox[0]
    for at in range(1, len(along_row) + 1):
        total += rowbox[at]
    mine[...] = total
    copies = []
    for k, device in along_col:
        copies.append(send(mine, colbox.at[col], sc, k, device))
    colbox[col] = total
    share_ref[...] = reduce_shares(pull_ref, inbox, rs, col, along_col, molecules)
    for copy in copies:
        copy.wait()
    total = colbox[0]
    for at in range(1, len(along_col) + 1):
        total += colbox[at]
    total_ref[...] = total


def prepare(dim, aux_ref, right, weights, lines):
    length = aux_ref.shape[0]
    piece = min(512, length)

    @pl.when(pl.program_id(0) == 0)
    def _():
        for start in range(0, length, piece):
            at = slice(start, start + piece)
            values = aux_ref[at, :]
            high, low = halves(values[:, :dim])
            right[at, :] = jnp.concatenate([high, low, high, low], axis=1).astype(jnp.bfloat16)
            ones = jnp.ones((piece, dim), jnp.float32)
            weights[at, :] = jnp.concatenate([high, low, ones, 0.0 * ones], axis=1).astype(jnp.bfloat16)
            lines[:, at] = values.T[dim : dim + 8]


def tile_kernel(first, chunk, dim, *refs):
    if first:
        rows_ref, cols_ref, arow_ref, acol_ref, dissim_ref, pull_ref, square_ref, right, weights, lines = refs
        rows = rows_ref[...]
    else:
        dissim_ref, arow_ref, acol_ref, pull_ref, square_ref, right, weights, lines = refs
    prepare(dim, acol_ref, right, weights, lines)
    tile, cols_len = dissim_ref.shape
    x = arow_ref[:, :dim]
    high, low = halves(x)
    left = (-2.0 * jnp.concatenate([high, high, low, low], axis=1)).astype(jnp.bfloat16)
    row_norm = arow_ref[:, dim : dim + 1]
    row_sq = arow_ref[:, dim + 1 : dim + 2]
    moved = jnp.zeros((tile, 4 * dim), jnp.float32)
    squares = jnp.zeros((tile, LANES), jnp.float32)
    contract = (((1,), (1,)), ((), ()))
    for start in range(0, cols_len, chunk):
        at = slice(start, start + chunk)
        if first:
            common = lax.dot_general(rows, cols_ref[at, :], contract, preferred_element_type=jnp.float32)
            dissim = 1.0 - common / ((row_sq + lines[1:2, at]) - common)
            dissim_ref[:, at] = dissim
        else:
            dissim = dissim_ref[:, at]
        cross = lax.dot_general(left, right[at, :], contract, preferred_element_type=jnp.float32)
        dist_sq = jnp.maximum((row_norm + lines[0:1, at]) + cross, FLOOR * FLOOR)
        inverse = lax.rsqrt(dist_sq)
        ratio = dissim * inverse
        gap = dissim if first else dissim - dist_sq * inverse
        squares += lanes_sum(gap * gap)
        top = ratio.astype(jnp.bfloat16)
        rest = (ratio - top.astype(jnp.float32)).astype(jnp.bfloat16)
        moved += jnp.dot(top, weights[at, :], preferred_element_type=jnp.float32)
        moved += jnp.dot(rest, weights[at, :], preferred_element_type=jnp.float32)
    pull = x * moved[:, 2 * dim : 2 * dim + 1] - (moved[:, :dim] + moved[:, dim : 2 * dim])
    stress = jnp.sum(squares, axis=1, keepdims=True)
    packed = jnp.concatenate([pull, jnp.broadcast_to(stress, (tile, LANES - dim))], axis=1)
    pull_ref[...] = packed.T[: pull_ref.shape[0]]
    square_ref[...] = rows_sum(squares)[None]


def on_device(features, coords):
    rows_n = lax.axis_size("row")
    cols_n = lax.axis_size("col")
    dim, share_len = coords.shape
    feat = features.shape[1]
    row_len = share_len * cols_n
    col_len = share_len * rows_n
    molecules = row_len * rows_n
    tile = 256
    chunk = 512
    steps = row_len // tile
    used = dim + 8
    big = 56 * 1024 * 1024
    f32 = jnp.float32
    any_spec = pl.BlockSpec(memory_space=pl.ANY)
    vmem = pl.BlockSpec(memory_space=pltpu.VMEM)
    dma = pltpu.SemaphoreType.DMA
    spread_sems = [dma((2, cols_n))] * 2 + [dma((2, rows_n // 2))] * 2

    def shape(*sizes, dtype=f32):
        return jax.ShapeDtypeStruct(sizes, dtype)

    def comm(number):
        return pltpu.CompilerParams(collective_id=number, has_side_effects=True, vmem_limit_bytes=big)

    wide = features.astype(f32)
    aux = with_norms(coords.T, jnp.sum(wide * wide, axis=1, keepdims=True))
    frows, fcols, arows, acols = pl.pallas_call(
        gather_kernel,
        in_specs=[any_spec, any_spec],
        out_specs=[any_spec] * 4,
        out_shape=[
            shape(cols_n, share_len, feat, dtype=features.dtype),
            shape(rows_n, share_len, feat, dtype=features.dtype),
            shape(cols_n, share_len, LANES),
            shape(rows_n, share_len, LANES),
        ],
        scratch_shapes=[dma((4,))] + spread_sems + spread_sems,
        compiler_params=comm(0),
    )(features, aux)

    by_row = lambda width: pl.BlockSpec((tile, width), lambda i: (i, 0))
    whole = lambda *sizes: pl.BlockSpec(sizes, lambda i: (0, 0))

    def tiles(first, *given):
        specs = [by_row(feat), whole(col_len, feat)] if first else [by_row(col_len)]
        outs = [pl.BlockSpec((used, tile), lambda i: (0, i)), pl.BlockSpec((1, 8, LANES), lambda i: (i, 0, 0))]
        shapes = [shape(used, row_len), shape(steps, 8, LANES)]
        if first:
            outs, shapes = [by_row(col_len)] + outs, [shape(row_len, col_len)] + shapes
        return pl.pallas_call(
            functools.partial(tile_kernel, first, chunk, dim),
            grid=(steps,),
            in_specs=specs + [by_row(LANES), whole(col_len, LANES)],
            out_specs=outs,
            out_shape=shapes,
            scratch_shapes=[
                pltpu.VMEM((col_len, 4 * dim), jnp.bfloat16),
                pltpu.VMEM((col_len, 4 * dim), jnp.bfloat16),
                pltpu.VMEM((8, col_len), f32),
            ],
            compiler_params=pltpu.CompilerParams(vmem_limit_bytes=big),
        )(*given)

    dissim, pull, dis_squares = tiles(
        True, frows.reshape(row_len, feat), fcols.reshape(col_len, feat),
        arows.reshape(row_len, LANES), acols.reshape(col_len, LANES),
    )
    inbox = pltpu.VMEM((cols_n, used, share_len), f32)
    boxes = [inbox, inbox, pltpu.VMEM((rows_n, used, share_len), f32), pltpu.VMEM((used, share_len), f32)]
    for sweep in range(1, ITERS):
        arows, acols = pl.pallas_call(
            functools.partial(turn_kernel, molecules, dim),
            in_specs=[vmem],
            out_specs=[vmem, vmem],
            out_shape=[shape(cols_n, share_len, LANES), shape(rows_n, share_len, LANES)],
            scratch_shapes=boxes + [dma((2, cols_n))] + spread_sems,
            compiler_params=comm(sweep),
        )(pull)
        pull, misfits = tiles(False, dissim, arows.reshape(row_len, LANES), acols.reshape(col_len, LANES))
    parts = jnp.stack([jnp.sum(misfits, axis=0), jnp.sum(dis_squares, axis=0)])
    share, totals = pl.pallas_call(
        functools.partial(last_kernel, molecules),
        in_specs=[vmem, vmem],
        out_specs=[vmem, vmem],
        out_shape=[shape(used, share_len), shape(2, 8, LANES)],
        scratch_shapes=[
            inbox, pltpu.VMEM((rows_n, 2, 8, LANES), f32), pltpu.VMEM((cols_n, 2, 8, LANES), f32),
            pltpu.VMEM((2, 8, LANES), f32), dma((2, cols_n)), dma((2, rows_n)), dma((2, cols_n)),
        ],
        compiler_params=comm(ITERS),
    )(pull, parts)
    totals = jnp.sum(totals, axis=(1, 2))
    return (share[:dim], share[dim], totals[0] / totals[1])


def solution(mesh):
    return jax.shard_map(
        on_device,
        mesh=mesh,
        in_specs=(P(("row", "col"), None), P(None, ("row", "col"))),
        out_specs=(P(None, ("row", "col")), P(("row", "col")), P()),
        check_vma=False,
    )
```

```python
import functools

import jax
import jax.numpy as jnp
from jax import lax
from jax.experimental import pallas as pl
from jax.experimental.pallas import tpu as pltpu
from jax.sharding import PartitionSpec as P

ITERS = 2
FLOOR = 0.25
LANES = 128
MESH = pl.DeviceIdType.MESH


def halves(x):
    high = lax.reduce_precision(x, 8, 7)
    return high, lax.reduce_precision(x - high, 8, 7)


def lanes_sum(values):
    total = values[:, :LANES]
    for at in range(LANES, values.shape[1], LANES):
        total += values[:, at : at + LANES]
    return total


def rows_sum(values):
    return jnp.sum(values.reshape(values.shape[0] // 8, 8, LANES), axis=0)


def with_norms(x, extra):
    length, dim = x.shape
    high, low = halves(x)
    hat = high + low
    norm = jnp.sum(hat * hat, axis=1, keepdims=True)
    lane = lax.broadcasted_iota(jnp.int32, (length, LANES - dim), 1)
    tail = jnp.where(lane == 0, norm, jnp.where(lane == 1, extra, 0.0))
    return jnp.concatenate([x, tail], axis=1)


def peers():
    row, col = lax.axis_index("row"), lax.axis_index("col")
    rows_n, cols_n = lax.axis_size("row"), lax.axis_size("col")
    along_row = [(k, (lax.rem(row + k, rows_n), col)) for k in range(1, rows_n)]
    along_col = [(k, (row, lax.rem(col + k, cols_n))) for k in range(1, cols_n)]
    return row, col, along_row, along_col


def greet(along_row, along_col):
    barrier = pltpu.get_barrier_semaphore()
    for _, device in along_row + along_col:
        pl.semaphore_signal(barrier, inc=1, device_id=device, device_id_type=MESH)
    pl.semaphore_wait(barrier, len(along_row) + len(along_col))


def send(source, target, sems, k, device):
    copy = pltpu.make_async_remote_copy(
        src_ref=source, dst_ref=target, send_sem=sems.at[0, k], recv_sem=sems.at[1, k],
        device_id=device, device_id_type=MESH,
    )
    copy.start()
    return copy


def link(source, target, sems, k, device):
    return pltpu.make_async_remote_copy(
        src_ref=source, dst_ref=target, send_sem=sems.at[0, k], recv_sem=sems.at[1, k],
        device_id=device, device_id_type=MESH,
    )


def spread(row, col, arrays):
    rows_n, cols_n = lax.axis_size("row"), lax.axis_size("col")
    chips = rows_n // 2
    chip, core = row // 2, lax.rem(row, 2)
    twin = (2 * chip + 1 - core, col)

    def inside(at):
        return (at >= 0) & (at < cols_n)

    def relay(array, t, step):
        source, by_col, _, sems = array
        slot = col - step * t
        return link(source if t == 0 else by_col.at[slot], by_col.at[slot],
                    sems[0] if step == 1 else sems[1], t, (row, col + step))

    def sends(t, step, act):
        @pl.when(inside(col - step * t) & inside(col + step))
        def _():
            for array in arrays:
                act(relay(array, t, step))

    def arrival(t, step):
        @pl.when(inside(col - step * (t + 1)))
        def _():
            for _, by_col, _, sems in arrays:
                slot = by_col.at[col - step * (t + 1)]
                link(slot, slot, sems[0] if step == 1 else sems[1], t, (row, col - step)).wait_recv()

    def cross(array, k):
        source, _, by_row, sems = array
        return link(source, by_row.at[row], sems[2], k, (2 * lax.rem(chip + k, chips) + core, col))

    def pass_on(array, k):
        source, _, by_row, sems = array
        slot = 2 * lax.rem(chip + chips - k, chips) + core
        return link(source if k == 0 else by_row.at[slot], by_row.at[slot], sems[3], k, twin)

    def forward(k):
        for array in arrays:
            cross(array, k).wait_recv()
            pass_on(array, k).start()

    for step in (1, -1):
        sends(0, step, lambda copy: copy.start())
    for k in range(1, chips):
        for array in arrays:
            cross(array, k).start()
    for array in arrays:
        pass_on(array, 0).start()
    for t in range(cols_n - 1):
        for step in (1, -1):
            arrival(t, step)
            if t + 1 < cols_n - 1:
                sends(t + 1, step, lambda copy: copy.start())
        if t + 1 < chips:
            forward(t + 1)
    for k in range(cols_n, chips):
        forward(k)
    for t in range(cols_n - 1):
        for step in (1, -1):
            sends(t, step, lambda copy: copy.wait_send())
    for array in arrays:
        for k in range(1, chips):
            cross(array, k).wait_send()
        for k in range(chips):
            pass_on(array, k).wait()


def gather_kernel(features_ref, aux_ref, frows_ref, fcols_ref, arows_ref, acols_ref, own, *sems):
    row, col, along_row, along_col = peers()
    local = []
    for at, (src, dst, place) in enumerate((
        (features_ref, frows_ref, col), (features_ref, fcols_ref, row),
        (aux_ref, arows_ref, col), (aux_ref, acols_ref, row),
    )):
        local.append(pltpu.make_async_copy(src, dst.at[place], own.at[at]))
        local[-1].start()
    greet(along_row, along_col)
    spread(row, col, [(features_ref, frows_ref, fcols_ref, sems[:4]), (aux_ref, arows_ref, acols_ref, sems[4:])])
    for copy in local:
        copy.wait()


def start_shares(pull_ref, inbox, sems, col, along_col):
    length = inbox.shape[2]
    share_of = lambda at: pl.ds(pl.multiple_of(at * length, LANES), length)
    copies = []
    for k, device in along_col:
        copies.append(send(pull_ref.at[:, share_of(device[1])], inbox.at[col], sems, k, device))
    inbox[col] = pull_ref[:, share_of(col)]
    return copies


def finish_shares(copies, inbox, molecules):
    for copy in copies:
        copy.wait()
    total = inbox[0]
    for at in range(1, inbox.shape[0]):
        total += inbox[at]
    return total / molecules


def turn_kernel(molecules, dim, pull_ref, arows_ref, acols_ref, inbox, rowsbox, colsbox, mine, rs, *sems):
    row, col, along_row, along_col = peers()
    greet(along_row, along_col)
    total = finish_shares(start_shares(pull_ref, inbox, rs, col, along_col), inbox, molecules)
    used, length = mine.shape
    mine[...] = with_norms(total[:dim].T, 0.0).T[:used]
    rowsbox[col] = mine[...]
    colsbox[row] = mine[...]
    spread(row, col, [(mine, rowsbox, colsbox, sems)])
    pad = jnp.zeros((LANES - used, length), jnp.float32)
    for box, out in ((rowsbox, arows_ref), (colsbox, acols_ref)):
        for at in range(box.shape[0]):
            out[at] = jnp.concatenate([box[at], pad], axis=0).T


def last_kernel(molecules, pull_ref, part_ref, share_ref, total_ref, inbox, rowbox, colbox, mine, rs, sr, sc):
    row, col, along_row, along_col = peers()
    greet(along_row, along_col)
    copies = []
    for k, device in along_row:
        copies.append(send(part_ref, rowbox.at[row], sr, k, device))
    rowbox[row] = part_ref[...]
    shares = start_shares(pull_ref, inbox, rs, col, along_col)
    for copy in copies:
        copy.wait()
    total = rowbox[0]
    for at in range(1, len(along_row) + 1):
        total += rowbox[at]
    mine[...] = total
    copies = []
    for k, device in along_col:
        copies.append(send(mine, colbox.at[col], sc, k, device))
    colbox[col] = total
    share_ref[...] = finish_shares(shares, inbox, molecules)
    for copy in copies:
        copy.wait()
    total = colbox[0]
    for at in range(1, len(along_col) + 1):
        total += colbox[at]
    total_ref[...] = total


def prepare(dim, aux_ref, right, weights, lines):
    length = aux_ref.shape[0]
    piece = min(512, length)

    @pl.when(pl.program_id(0) == 0)
    def _():
        for start in range(0, length, piece):
            at = slice(start, start + piece)
            values = aux_ref[at, :]
            high, low = halves(values[:, :dim])
            right[at, :] = jnp.concatenate([high, low, high, low], axis=1).astype(jnp.bfloat16)
            ones = jnp.ones((piece, dim), jnp.float32)
            weights[at, :] = jnp.concatenate([high, low, ones, 0.0 * ones], axis=1).astype(jnp.bfloat16)
            lines[:, at] = values.T[dim : dim + 8]


def tile_kernel(first, chunk, dim, *refs):
    if first:
        rows_ref, cols_ref, arow_ref, acol_ref, dissim_ref, pull_ref, square_ref, right, weights, lines = refs
        rows = rows_ref[...]
    else:
        dissim_ref, arow_ref, acol_ref, pull_ref, square_ref, right, weights, lines = refs
    prepare(dim, acol_ref, right, weights, lines)
    tile, cols_len = dissim_ref.shape
    x = arow_ref[:, :dim]
    high, low = halves(x)
    left = (-2.0 * jnp.concatenate([high, high, low, low], axis=1)).astype(jnp.bfloat16)
    row_norm = arow_ref[:, dim : dim + 1]
    row_sq = arow_ref[:, dim + 1 : dim + 2]
    moved = jnp.zeros((tile, 4 * dim), jnp.float32)
    squares = jnp.zeros((tile, LANES), jnp.float32)
    contract = (((1,), (1,)), ((), ()))
    for start in range(0, cols_len, chunk):
        at = slice(start, start + chunk)
        if first:
            common = lax.dot_general(rows, cols_ref[at, :], contract, preferred_element_type=jnp.float32)
            dissim = 1.0 - common / ((row_sq + lines[1:2, at]) - common)
            dissim_ref[:, at] = dissim
        else:
            dissim = dissim_ref[:, at]
        cross = lax.dot_general(left, right[at, :], contract, preferred_element_type=jnp.float32)
        dist_sq = jnp.maximum((row_norm + lines[0:1, at]) + cross, FLOOR * FLOOR)
        inverse = lax.rsqrt(dist_sq)
        ratio = dissim * inverse
        gap = dissim if first else dissim - dist_sq * inverse
        squares += lanes_sum(gap * gap)
        top = ratio.astype(jnp.bfloat16)
        rest = (ratio - top.astype(jnp.float32)).astype(jnp.bfloat16)
        moved += jnp.dot(top, weights[at, :], preferred_element_type=jnp.float32)
        moved += jnp.dot(rest, weights[at, :], preferred_element_type=jnp.float32)
    pull = x * moved[:, 2 * dim : 2 * dim + 1] - (moved[:, :dim] + moved[:, dim : 2 * dim])
    stress = jnp.sum(squares, axis=1, keepdims=True)
    packed = jnp.concatenate([pull, jnp.broadcast_to(stress, (tile, LANES - dim))], axis=1)
    pull_ref[...] = packed.T[: pull_ref.shape[0]]
    square_ref[...] = rows_sum(squares)[None]


def on_device(features, coords):
    rows_n = lax.axis_size("row")
    cols_n = lax.axis_size("col")
    dim, share_len = coords.shape
    feat = features.shape[1]
    row_len = share_len * cols_n
    col_len = share_len * rows_n
    molecules = row_len * rows_n
    tile = 256
    chunk = 512
    steps = row_len // tile
    used = dim + 8
    big = 56 * 1024 * 1024
    f32 = jnp.float32
    any_spec = pl.BlockSpec(memory_space=pl.ANY)
    vmem = pl.BlockSpec(memory_space=pltpu.VMEM)
    dma = pltpu.SemaphoreType.DMA
    spread_sems = [dma((2, cols_n))] * 2 + [dma((2, rows_n // 2))] * 2

    def shape(*sizes, dtype=f32):
        return jax.ShapeDtypeStruct(sizes, dtype)

    def comm(number):
        return pltpu.CompilerParams(collective_id=number, has_side_effects=True, vmem_limit_bytes=big)

    wide = features.astype(f32)
    aux = with_norms(coords.T, jnp.sum(wide * wide, axis=1, keepdims=True))
    frows, fcols, arows, acols = pl.pallas_call(
        gather_kernel,
        in_specs=[any_spec, any_spec],
        out_specs=[any_spec] * 4,
        out_shape=[
            shape(cols_n, share_len, feat, dtype=features.dtype),
            shape(rows_n, share_len, feat, dtype=features.dtype),
            shape(cols_n, share_len, LANES),
            shape(rows_n, share_len, LANES),
        ],
        scratch_shapes=[dma((4,))] + spread_sems + spread_sems,
        compiler_params=comm(0),
    )(features, aux)

    by_row = lambda width: pl.BlockSpec((tile, width), lambda i: (i, 0))
    whole = lambda *sizes: pl.BlockSpec(sizes, lambda i: (0, 0))

    def tiles(first, *given):
        specs = [by_row(feat), whole(col_len, feat)] if first else [by_row(col_len)]
        outs = [pl.BlockSpec((used, tile), lambda i: (0, i)), pl.BlockSpec((1, 8, LANES), lambda i: (i, 0, 0))]
        shapes = [shape(used, row_len), shape(steps, 8, LANES)]
        if first:
            outs, shapes = [by_row(col_len)] + outs, [shape(row_len, col_len)] + shapes
        return pl.pallas_call(
            functools.partial(tile_kernel, first, chunk, dim),
            grid=(steps,),
            in_specs=specs + [by_row(LANES), whole(col_len, LANES)],
            out_specs=outs,
            out_shape=shapes,
            scratch_shapes=[
                pltpu.VMEM((col_len, 4 * dim), jnp.bfloat16),
                pltpu.VMEM((col_len, 4 * dim), jnp.bfloat16),
                pltpu.VMEM((8, col_len), f32),
            ],
            compiler_params=pltpu.CompilerParams(vmem_limit_bytes=big),
        )(*given)

    dissim, pull, dis_squares = tiles(
        True, frows.reshape(row_len, feat), fcols.reshape(col_len, feat),
        arows.reshape(row_len, LANES), acols.reshape(col_len, LANES),
    )
    inbox = pltpu.VMEM((cols_n, used, share_len), f32)
    boxes = [inbox, inbox, pltpu.VMEM((rows_n, used, share_len), f32), pltpu.VMEM((used, share_len), f32)]
    for sweep in range(1, ITERS):
        arows, acols = pl.pallas_call(
            functools.partial(turn_kernel, molecules, dim),
            in_specs=[vmem],
            out_specs=[vmem, vmem],
            out_shape=[shape(cols_n, share_len, LANES), shape(rows_n, share_len, LANES)],
            scratch_shapes=boxes + [dma((2, cols_n))] + spread_sems,
            compiler_params=comm(sweep),
        )(pull)
        pull, misfits = tiles(False, dissim, arows.reshape(row_len, LANES), acols.reshape(col_len, LANES))
    parts = jnp.stack([jnp.sum(misfits, axis=0), jnp.sum(dis_squares, axis=0)])
    share, totals = pl.pallas_call(
        functools.partial(last_kernel, molecules),
        in_specs=[vmem, vmem],
        out_specs=[vmem, vmem],
        out_shape=[shape(used, share_len), shape(2, 8, LANES)],
        scratch_shapes=[
            inbox, pltpu.VMEM((rows_n, 2, 8, LANES), f32), pltpu.VMEM((cols_n, 2, 8, LANES), f32),
            pltpu.VMEM((2, 8, LANES), f32), dma((2, cols_n)), dma((2, rows_n)), dma((2, cols_n)),
        ],
        compiler_params=comm(ITERS),
    )(pull, parts)
    totals = jnp.sum(totals, axis=(1, 2))
    return (share[:dim], share[dim], totals[0] / totals[1])


def solution(mesh):
    return jax.shard_map(
        on_device,
        mesh=mesh,
        in_specs=(P(("row", "col"), None), P(None, ("row", "col"))),
        out_specs=(P(None, ("row", "col")), P(("row", "col")), P()),
        check_vma=False,
    )
```
